32 devices in a mesh: group: 2 (over x), tm: 16 (over z, y, core).
Axes of the slice: x: 2, y: 2, z: 4, core: 2. Of those that a mesh axis runs over, the one named last changes fastest.
Arguments:
- obs_blocks: bfloat16 [32, 512, 64, 128], P(('group', 'tm')), parts along dimension 0, may hold values from -0.5 to 0.5
- block_rows: int32 [32, 512], P(('group', 'tm')), parts along dimension 0, may hold values from 0 to 511
- block_cols: int32 [32, 512], P(('group', 'tm')), parts along dimension 0, may hold values from 0 to 15
- block_count: int32 [32], P(('group', 'tm')), parts along dimension 0, may hold values from 256 to 512, as said below
- background: bfloat16 [32, 16, 2048], P(('group', 'tm')), parts along dimension 0, may hold values from -6 to 6
- observed: float32 [32, 16, 32768], P(('group', 'tm')), parts along dimension 0, may hold values from -6 to 6
- obs_weight: float32 [32, 32768], P(('group', 'tm')), parts along dimension 0, may hold values from 0.01 to 0.1
- info_diag: float32 [32, 2048], P(('group', 'tm')), parts along dimension 0, may hold values from 0.003 to 0.03
- decay: float32 [32, 2048], P(('group', 'tm')), parts along dimension 0, may hold values from 0.5 to 1
- noise_var: float32 [32, 2048], P(('group', 'tm')), parts along dimension 0, may hold values from 0.003 to 0.03
- prior_var: float32 [4096], P('group'), parts along dimension 0, may hold values from 0.5 to 2
Outputs:
- smooth_mean: float32 [32, 16, 2048], P(('group', 'tm')), parts along dimension 0
- smooth_var: float32 [32, 2048], P(('group', 'tm')), parts along dimension 0
The draws below stay inside these ranges and needn't reach their ends.
There are 2 independent parts, one for each index of `group`. The reference program is written for one: setup_inputs(seed, part) draws one part's arguments, and reference() takes and returns one part's arrays. A program takes and returns all parts, laid end to end along the dimension named above; each array names one. Nothing has to cross between parts.
Inputs may be any that keep to these rules, and one draw needn't show every extreme that they name: Blocks 0 to block_count[t] - 1 of step t are in use; some step uses all 512 blocks and some step exactly half of them.
All inputs are finite; a program needn't handle non-finite values.
Results may differ from the reference program's by a relative error of at most 0.0045.
Values sent between devices are 32-bit elements; how exact they have to be, the bound alone decides.
A program may use at most 64 MiB of HBM per device.

```python
import math
import jax
import jax.numpy as jnp
from jax import lax

N = 2048
CB = 128
RB = 64
NB = 512
MEM = 16
CLOCK_INTERVALS = 16


def draw_block_count(key, part):
    key_counts = jax.random.fold_in(key, 11)
    key_first = jax.random.fold_in(key, 12)
    key_second = jax.random.fold_in(key, 13)
    counts = jax.random.randint(key_counts, (CLOCK_INTERVALS,), NB // 2, NB + 1)
    first_spot = jax.random.randint(key_first, (), 0, CLOCK_INTERVALS)
    second_spot = (first_spot + 1 + jax.random.randint(key_second, (), 0, CLOCK_INTERVALS - 1)) % CLOCK_INTERVALS
    positions = jnp.arange(CLOCK_INTERVALS)
    counts = jnp.where(positions == first_spot, NB, counts)
    counts = jnp.where(positions == second_spot, NB // 2, counts)
    return counts.astype(jnp.int32)


def draw_decay(key, part):
    key_rates = jax.random.fold_in(key, 21)
    key_rough = jax.random.fold_in(key, 22)
    lookup_location_array = jax.random.fold_in(key, 23)
    key_kept = jax.random.fold_in(key, 24)
    incoming_frequency = jnp.exp(jax.random.uniform(key_rates, (1, N), jnp.float32, math.log(0.5 / CLOCK_INTERVALS), math.log(1.0 / 30.0)))
    terrain_unevenness = jax.random.uniform(key_rough, (CLOCK_INTERVALS, N), jnp.float32, 0.5, 1.5)
    pulse_location_array = jax.random.randint(lookup_location_array, (4,), 0, CLOCK_INTERVALS)
    live_pulse_events = jnp.any(jnp.arange(CLOCK_INTERVALS)[:, None] == pulse_location_array[None, :], axis=1)
    preserved_proportion = jax.random.uniform(key_kept, (CLOCK_INTERVALS, N), jnp.float32, 0.5, 0.8)
    return jnp.where(live_pulse_events[:, None], preserved_proportion, jnp.exp(-incoming_frequency * terrain_unevenness)).astype(jnp.float32)


def touch_ends(values, rng, least, top_value):
    longest = values.shape.index(max(values.shape))
    spots = []
    for shift in (0, 1):
        where = [jax.random.randint(jax.random.fold_in(rng, axis), (), 0, length) for axis, length in enumerate(values.shape)]
        where[longest] = (where[longest] + shift) % values.shape[longest]
        spots.append(tuple(where))
    return values.at[spots[0]].set(least).at[spots[1]].set(top_value)


def level_of(key, shape, pieces, low, high):
    level = 1.0
    for axis_at, parts in pieces:
        draws = jax.random.uniform(jax.random.fold_in(jax.random.fold_in(key, 6), axis_at), (parts,), jnp.float32, low / len(pieces), high / len(pieces))
        level = level * jnp.repeat(jnp.exp(draws), shape[axis_at] // parts).reshape((-1,) + (1,) * (len(shape) - 1 - axis_at))
    return level


def gaussian(stream_key, shape, width, reach, shards=(), dtype=jnp.bfloat16):
    drawn = jax.random.normal(stream_key, shape, jnp.float32) * width
    if len(shards) > 0:
        drawn = level_of(stream_key, shape, shards, -0.22, 0.18) * drawn
    return jnp.clip(drawn, min=-reach, max=reach).astype(dtype)


def setup_inputs(seed: int = 0, part: int = 0) -> dict:
    key_list = jax.random.split(jax.random.key(seed), 12)
    part_splits = jax.random.split(jax.random.fold_in(key_list[11], part), 12)
    return {
        "obs_blocks": gaussian(part_splits[0], (CLOCK_INTERVALS, NB, RB, CB), CB ** -0.5, 0.5, ((0, 16),)),
        "block_rows": touch_ends(jax.random.randint(part_splits[1], (CLOCK_INTERVALS, NB), 0, NB), jax.random.fold_in(part_splits[1], 1), 0, NB - 1).astype(jnp.int32),
        "block_cols": touch_ends(jax.random.randint(part_splits[2], (CLOCK_INTERVALS, NB), 0, N // CB), jax.random.fold_in(part_splits[2], 1), 0, (N // CB) - 1).astype(jnp.int32),
        "block_count": draw_block_count(jax.random.fold_in(jax.random.fold_in(key_list[11], part), 71), part),
        "background": gaussian(part_splits[4], (CLOCK_INTERVALS, MEM, N), 1.0, 6.0, ((0, 16),)),
        "observed": gaussian(part_splits[5], (CLOCK_INTERVALS, MEM, NB * RB), 1.0, 6.0, ((0, 16),), jnp.float32),
        "obs_weight": jnp.clip(jnp.exp(math.log(0.1) - 2.3025851 * jax.random.uniform(part_splits[6], (CLOCK_INTERVALS, NB * RB), jnp.float32) ** level_of(part_splits[6], (CLOCK_INTERVALS, NB * RB), ((0, 16),), -0.2, 0.2)), 0.01, 0.1),
        "info_diag": jnp.clip(jnp.exp(math.log(0.03) - 2.3025851 * jax.random.uniform(part_splits[7], (CLOCK_INTERVALS, N), jnp.float32) ** level_of(part_splits[7], (CLOCK_INTERVALS, N), ((0, 16),), -0.2, 0.2)), 0.003, 0.03),
        "decay": draw_decay(jax.random.fold_in(jax.random.fold_in(key_list[11], part), 71), part),
        "noise_var": jnp.clip(jnp.exp(math.log(0.03) - 2.3025851 * jax.random.uniform(part_splits[9], (CLOCK_INTERVALS, N), jnp.float32) ** level_of(part_splits[9], (CLOCK_INTERVALS, N), ((0, 16),), -0.2, 0.2)), 0.003, 0.03),
        "prior_var": jnp.clip(jnp.exp(jax.random.uniform(part_splits[10], (N,), jnp.float32, math.log(0.5), math.log(2.0))), 0.5, 2.0),
    }


def step_gradient(inputs):
    blocks_here, rows_here, cols_here, count_here, back_here, seen_here, weight_here = inputs
    block_total, row_size, col_size = blocks_here.shape
    member_total = back_here.shape[0]
    group_total = back_here.shape[1] // col_size
    row_total = seen_here.shape[1] // row_size
    active = (jnp.arange(block_total) < count_here).astype(jnp.float32)
    col_onehot = (cols_here[:, None] == jnp.arange(group_total)[None, :]).astype(jnp.float32)
    row_indicator = (rows_here[:, None] == jnp.arange(row_total)[None, :]).astype(jnp.float32) * active[:, None]
    states = back_here.astype(jnp.float32).reshape(member_total, group_total, col_size)
    block_values = blocks_here.astype(jnp.float32)
    picked = jnp.einsum("bk,mkc->mbc", col_onehot, states, precision=lax.Precision.HIGHEST)
    applied_result = jnp.einsum("bic,mbc->mbi", block_values, picked, precision=lax.Precision.HIGHEST)
    mapped_images = jnp.einsum("br,mbi->mri", row_indicator, applied_result, precision=lax.Precision.HIGHEST)
    mapped_images = mapped_images.reshape(member_total, row_total * row_size)
    weighted = (weight_here[None, :] * (seen_here - mapped_images)).reshape(member_total, row_total, row_size)
    rows_back = jnp.einsum("br,mri->mbi", row_indicator, weighted, precision=lax.Precision.HIGHEST)
    rows_back = lax.optimization_barrier(rows_back.astype(jnp.bfloat16)).astype(jnp.float32)
    pulled = jnp.einsum("bic,mbi->mbc", block_values, rows_back, precision=lax.Precision.HIGHEST)
    gradient = jnp.einsum("bk,mbc->mkc", col_onehot, pulled, precision=lax.Precision.HIGHEST)
    return gradient.reshape(member_total, group_total * col_size)


def reference(obs_blocks, block_rows, block_cols, block_count, background, observed, obs_weight, info_diag, decay, noise_var, prior_var):
    gradient = lax.map(step_gradient, (obs_blocks, block_rows, block_cols, block_count, background, observed, obs_weight))
    member_total = gradient.shape[1]
    step_ids = jnp.arange(CLOCK_INTERVALS)
    is_first = step_ids == 0
    is_final = step_ids == CLOCK_INTERVALS - 1

    def forward(carried, inputs):
        mean_prev, var_prev = carried
        grad_now, info_now, decay_now, noise_now, first_now = inputs
        pred_var = jnp.where(first_now, prior_var, decay_now * decay_now * var_prev + noise_now)
        pred_mean = jnp.where(first_now, 0.0, decay_now * mean_prev)
        var_now = pred_var / (1.0 + info_now * pred_var)
        mean_now = var_now * (pred_mean / pred_var + grad_now)
        return (mean_now, var_now), (mean_now, var_now)

    initial = (jnp.zeros((member_total, N), jnp.float32), jnp.ones((N,), jnp.float32))
    filtered = lax.scan(forward, initial, (gradient, info_diag, decay, noise_var, is_first))[1]
    means, variances = filtered
    next_decay = jnp.concatenate([decay[1:], jnp.zeros((1, N), jnp.float32)], axis=0)
    next_noise = jnp.concatenate([noise_var[1:], jnp.ones((1, N), jnp.float32)], axis=0)

    def backward(carried, inputs):
        later_mean, later_var = carried
        mean_now, var_now, decay_next, noise_next, final_now = inputs
        pred_var = decay_next * decay_next * var_now + noise_next
        smoother_gain = jnp.where(final_now, 0.0, var_now * decay_next / pred_var)
        out_mean = mean_now + smoother_gain * (later_mean - decay_next * mean_now)
        out_var = var_now + smoother_gain * smoother_gain * (later_var - pred_var)
        return (out_mean, out_var), (out_mean, out_var)

    closing = (jnp.zeros((member_total, N), jnp.float32), jnp.zeros((N,), jnp.float32))
    smoothed = lax.scan(backward, closing, (means, variances, next_decay, next_noise, is_final), reverse=True)[1]
    return smoothed[0], smoothed[1]
```

```python
import functools

import jax
import jax.numpy as jnp
from jax import lax
from jax.experimental import pallas as pl
from jax.experimental.pallas import tpu as pltpu
from jax.sharding import PartitionSpec as P

MESH = pl.DeviceIdType.MESH
CHUNKS = 8
GROUP = 4


def gradient_kernel(
    rows, cols, count, back_ref, weight_ref, blocks_hbm, observed_hbm,
    out_ref, states, blocks, misfit, block_sems, observed_sem,
):
    block_total = rows.shape[1]
    row_size = blocks.shape[0] // block_total
    members = back_ref.shape[1]
    state_total, _, col_size = states.shape
    chunk = block_total // CHUNKS

    observed_copy = pltpu.make_async_copy(observed_hbm, misfit, observed_sem)
    observed_copy.start()
    copies = []
    for part in range(CHUNKS):
        span = pl.ds(part * chunk * row_size, chunk * row_size)
        copies.append(
            pltpu.make_async_copy(blocks_hbm.at[span], blocks.at[span], block_sems.at[part])
        )
        copies[-1].start()

    for k in range(state_total):
        states[k] = back_ref[0, :, k * col_size:(k + 1) * col_size]
    out_ref[...] = jnp.zeros_like(out_ref)
    lane_half = lax.broadcasted_iota(jnp.int32, (members, 2 * row_size), 1) // row_size
    in_use = count[0]
    observed_copy.wait()

    def place(row):
        return pl.ds(pl.multiple_of((row // 2) * 2 * row_size, 2 * row_size), 2 * row_size)

    def apply_group(group, _):
        first = group * GROUP
        picked = jnp.concatenate([states[cols[0, first + j]] for j in range(GROUP)], axis=0)
        tile = blocks[pl.ds(pl.multiple_of(first * row_size, GROUP * row_size), GROUP * row_size), :]
        applied = lax.dot_general(
            picked, tile, (((1,), (1,)), ((), ())), preferred_element_type=jnp.float32
        )
        for j in range(GROUP):
            row = rows[0, first + j]
            half = row % 2
            piece = applied[
                j * members:(j + 1) * members,
                (j // 2) * 2 * row_size:(j // 2 + 1) * 2 * row_size,
            ]
            piece = pltpu.roll(piece, (half ^ (j % 2)) * row_size, 1)
            wanted = jnp.where(first + j < in_use, half, 2)
            at = place(row)
            misfit[:, at] = misfit[:, at] - jnp.where(lane_half == wanted, piece, 0.0)
        return 0

    for part in range(CHUNKS):
        copies[part].wait()
        per = chunk // GROUP
        lax.fori_loop(part * per, (part + 1) * per, apply_group, 0, unroll=4)

    def pull_group(group, _):
        first = group * GROUP
        pieces = []
        for j in range(GROUP):
            row = rows[0, first + j]
            at = place(row)
            value = misfit[:, at] * weight_ref[:, at]
            value = pltpu.roll(value, ((row % 2) ^ (j % 2)) * row_size, 1)
            wanted = jnp.where(first + j < in_use, j % 2, 2)
            value = jnp.where(lane_half == wanted, value, 0.0).astype(jnp.bfloat16)
            nothing = jnp.zeros_like(value)
            pieces.append(
                jnp.concatenate([value if s == j // 2 else nothing for s in range(GROUP // 2)], axis=1)
            )
        tile = blocks[pl.ds(pl.multiple_of(first * row_size, GROUP * row_size), GROUP * row_size), :]
        pulled = jnp.dot(
            jnp.concatenate(pieces, axis=0), tile, preferred_element_type=jnp.float32
        )
        for j in range(GROUP):
            k = cols[0, first + j]
            out_ref[k] = out_ref[k] + pulled[j * members:(j + 1) * members]
        return 0

    lax.fori_loop(0, block_total // GROUP, pull_group, 0, unroll=4)


def gradients(obs_blocks, block_rows, block_cols, block_count, background, observed, obs_weight):
    _, block_total, row_size, col_size = obs_blocks.shape
    members = background.shape[1]
    state_total = background.shape[2] // col_size
    smem = pl.BlockSpec(memory_space=pltpu.SMEM)
    vmem = pl.BlockSpec(memory_space=pltpu.VMEM)
    hbm = pl.BlockSpec(memory_space=pltpu.HBM)
    return pl.pallas_call(
        gradient_kernel,
        out_shape=jax.ShapeDtypeStruct((state_total, members, col_size), jnp.float32),
        in_specs=[smem, smem, smem, vmem, vmem, hbm, hbm],
        out_specs=vmem,
        scratch_shapes=[
            pltpu.VMEM((state_total, members, col_size), jnp.bfloat16),
            pltpu.VMEM((block_total * row_size, col_size), jnp.bfloat16),
            pltpu.VMEM((members, observed.shape[2]), jnp.float32),
            pltpu.SemaphoreType.DMA((CHUNKS,)),
            pltpu.SemaphoreType.DMA,
        ],
        compiler_params=pltpu.CompilerParams(vmem_limit_bytes=62 * 2**20),
        name="local_gradient",
    )(
        block_rows, block_cols, block_count, background, obs_weight,
        obs_blocks.reshape(block_total * row_size, col_size),
        observed.reshape(members, observed.shape[2]),
    )


def smoother_kernel(
    n, grad_ref, info_ref, decay_ref, noise_ref, prior_ref, mean_out, var_out,
    coef_send, coef_recv, grad_recv, mean_send, var_send,
    coef_ss, coef_rs, grad_ss, grad_rs, mean_ss, mean_rs, var_ss, var_rs,
):
    me = lax.axis_index("tm")
    width = coef_send.shape[2]

    barrier = pltpu.get_barrier_semaphore()

    def greet(d, _):
        pl.semaphore_signal(
            barrier, inc=1, device_id={"tm": lax.rem(me + d, n)}, device_id_type=MESH
        )
        return 0

    lax.fori_loop(1, n, greet, 0)
    for k in range(n):
        columns = slice(k * width, (k + 1) * width)
        coef_send[k, 0:1, :] = info_ref[:, columns]
        coef_send[k, 1:2, :] = decay_ref[:, columns]
        coef_send[k, 2:3, :] = noise_ref[:, columns]
    mine = pl.ds(pl.multiple_of(me * width, width), width)
    coef_recv[me] = coef_send[me]
    grad_recv[me] = grad_ref[me]
    pl.semaphore_wait(barrier, n - 1)

    def remote(src, dst, send_sem, recv_sem, d):
        to = lax.rem(me + d, n)
        return pltpu.make_async_remote_copy(
            src_ref=src(to), dst_ref=dst(me), send_sem=send_sem.at[to], recv_sem=recv_sem.at[me],
            device_id={"tm": to}, device_id_type=MESH,
        )

    def arrival(src, dst, send_sem, recv_sem, d):
        other = lax.rem(me + d, n)
        return pltpu.make_async_remote_copy(
            src_ref=src(other), dst_ref=dst(other), send_sem=send_sem.at[other],
            recv_sem=recv_sem.at[other], device_id={"tm": other}, device_id_type=MESH,
        )

    def start_all(*what):
        def body(d, _):
            remote(*what, d).start()
            return 0
        lax.fori_loop(1, n, body, 0)

    def wait_all(*what):
        def body(d, _):
            arrival(*what, d).wait_recv()
            return 0
        lax.fori_loop(1, n, body, 0)

    def sent_all(*what):
        def body(d, _):
            remote(*what, d).wait_send()
            return 0
        lax.fori_loop(1, n, body, 0)

    def columns_of(ref):
        return lambda k: ref.at[:, pl.ds(pl.multiple_of(k * width, width), width)]

    coefs = (lambda k: coef_send.at[k], lambda k: coef_recv.at[k], coef_ss, coef_rs)
    grads = (lambda k: grad_ref.at[k], lambda k: grad_recv.at[k], grad_ss, grad_rs)
    means = (lambda k: mean_send.at[k], columns_of(mean_out), mean_ss, mean_rs)
    varis = (lambda k: var_send.at[k], columns_of(var_out), var_ss, var_rs)

    start_all(*coefs)
    start_all(*grads)
    wait_all(*coefs)

    info = [coef_recv[t, 0:1, :] for t in range(n)]
    decay = [coef_recv[t, 1:2, :] for t in range(n)]
    noise = [coef_recv[t, 2:3, :] for t in range(n)]
    var, carry = [], []
    for t in range(n):
        if t == 0:
            pred = prior_ref[:, mine]
            carry.append(None)
        else:
            pred = decay[t] * decay[t] * var[t - 1] + noise[t]
        scale = 1.0 / (1.0 + info[t] * pred)
        var.append(pred * scale)
        if t > 0:
            carry.append(scale * decay[t])
    gain = []
    later = [None] * n
    later[n - 1] = var[n - 1]
    for t in range(n - 1):
        pred = decay[t + 1] * decay[t + 1] * var[t] + noise[t + 1]
        gain.append(var[t] * decay[t + 1] / pred)
    for t in range(n - 2, -1, -1):
        pred = decay[t + 1] * decay[t + 1] * var[t] + noise[t + 1]
        later[t] = var[t] + gain[t] * gain[t] * (later[t + 1] - pred)
    for t in range(n):
        var_send[t] = later[t]
    start_all(*varis)
    var_out[:, mine] = var_send[me]

    wait_all(*grads)
    mean = []
    for t in range(n):
        now = var[t] * grad_recv[t]
        mean.append(now if t == 0 else carry[t] * mean[t - 1] + now)
    smooth = mean[n - 1]
    mean_send[n - 1] = smooth
    for t in range(n - 2, -1, -1):
        smooth = mean[t] + gain[t] * (smooth - decay[t + 1] * mean[t])
        mean_send[t] = smooth
    start_all(*means)
    mean_out[:, mine] = mean_send[me]

    wait_all(*varis)
    wait_all(*means)
    sent_all(*coefs)
    sent_all(*grads)
    sent_all(*varis)
    sent_all(*means)


def exchange_and_smooth(n, gradient, info_diag, decay, noise_var, prior_var):
    state_total, members, width = gradient.shape
    total = state_total * width
    vmem = pl.BlockSpec(memory_space=pltpu.VMEM)
    mean, var = pl.pallas_call(
        functools.partial(smoother_kernel, n),
        out_shape=(
            jax.ShapeDtypeStruct((members, total), jnp.float32),
            jax.ShapeDtypeStruct((1, total), jnp.float32),
        ),
        in_specs=[vmem] * 5,
        out_specs=(vmem, vmem),
        scratch_shapes=[
            pltpu.VMEM((n, 3, width), jnp.float32),
            pltpu.VMEM((n, 3, width), jnp.float32),
            pltpu.VMEM((n, members, width), jnp.float32),
            pltpu.VMEM((n, members, width), jnp.float32),
            pltpu.VMEM((n, 1, width), jnp.float32),
        ] + [pltpu.SemaphoreType.DMA((n,))] * 8,
        compiler_params=pltpu.CompilerParams(collective_id=0, has_side_effects=True),
        name="exchange_smooth",
    )(gradient, info_diag, decay, noise_var, prior_var.reshape(1, total))
    return mean[None], var


def sequential_smoother(series, prior_here, member_total):
    full_steps = series.shape[0]
    grad_all = series[:, :member_total, :]
    info_all = series[:, member_total, :]
    decay_all = series[:, member_total + 1, :]
    noise_all = series[:, member_total + 2, :]
    local_width = series.shape[2]
    step_ids = jnp.arange(full_steps)
    first_flags = step_ids == 0
    final_flags = step_ids == full_steps - 1

    def forward(carried, inputs):
        mean_prev, var_prev = carried
        grad_now, info_now, decay_now, noise_now, first_now = inputs
        pred_var = jnp.where(first_now, prior_here, decay_now * decay_now * var_prev + noise_now)
        pred_mean = jnp.where(first_now, 0.0, decay_now * mean_prev)
        var_now = pred_var / (1.0 + info_now * pred_var)
        mean_now = var_now * (pred_mean / pred_var + grad_now)
        return ((mean_now, var_now), (mean_now, var_now))

    initial = (
        jnp.zeros((member_total, local_width), jnp.float32),
        jnp.ones((local_width,), jnp.float32),
    )
    means, variances = lax.scan(
        forward, initial, (grad_all, info_all, decay_all, noise_all, first_flags)
    )[1]
    next_decay = jnp.concatenate([decay_all[1:], jnp.zeros((1, local_width), jnp.float32)], axis=0)
    next_noise = jnp.concatenate([noise_all[1:], jnp.ones((1, local_width), jnp.float32)], axis=0)

    def backward(carried, inputs):
        later_mean, later_var = carried
        mean_now, var_now, decay_next, noise_next, final_now = inputs
        pred_var = decay_next * decay_next * var_now + noise_next
        smoother_gain = jnp.where(final_now, 0.0, var_now * decay_next / pred_var)
        out_mean = mean_now + smoother_gain * (later_mean - decay_next * mean_now)
        out_var = var_now + smoother_gain * smoother_gain * (later_var - pred_var)
        return ((out_mean, out_var), (out_mean, out_var))

    closing = (
        jnp.zeros((member_total, local_width), jnp.float32),
        jnp.zeros((local_width,), jnp.float32),
    )
    return lax.scan(
        backward, closing, (means, variances, next_decay, next_noise, final_flags), reverse=True
    )[1]


def shards(
    obs_blocks,
    block_rows,
    block_cols,
    block_count,
    background,
    observed,
    obs_weight,
    info_diag,
    decay,
    noise_var,
    prior_var,
):
    member_total = background.shape[1]
    state_total = background.shape[2]
    n = lax.axis_size("tm")
    gradient = gradients(
        obs_blocks, block_rows, block_cols, block_count, background, observed, obs_weight
    )
    local_width = state_total // n
    if local_width == gradient.shape[2]:
        return exchange_and_smooth(n, gradient, info_diag, decay, noise_var, prior_var)
    gradient = jnp.transpose(gradient, (1, 0, 2)).reshape(1, member_total, state_total)
    packed = jnp.concatenate(
        [gradient, info_diag[:, None, :], decay[:, None, :], noise_var[:, None, :]], axis=1
    )
    series = lax.all_to_all(packed, "tm", split_axis=2, concat_axis=0, tiled=True)
    prior_here = lax.dynamic_slice_in_dim(
        prior_var, lax.axis_index("tm") * local_width, local_width, 0
    )
    mean_series, var_series = sequential_smoother(series, prior_here, member_total)
    outgoing = jnp.concatenate([mean_series, var_series[:, None, :]], axis=1)
    returned = lax.all_to_all(outgoing, "tm", split_axis=0, concat_axis=2, tiled=True)
    return (returned[:, :member_total, :], returned[:, member_total, :])


def solution(mesh):
    in_specs = (
        P(("group", "tm"), None, None, None),
        P(("group", "tm"), None),
        P(("group", "tm"), None),
        P(("group", "tm")),
        P(("group", "tm"), None, None),
        P(("group", "tm"), None, None),
        P(("group", "tm"), None),
        P(("group", "tm"), None),
        P(("group", "tm"), None),
        P(("group", "tm"), None),
        P("group"),
    )
    out_specs = (P(("group", "tm"), None, None), P(("group", "tm"), None))
    return jax.shard_map(shards, mesh=mesh, in_specs=in_specs, out_specs=out_specs, check_vma=False)
```

```python
import functools

import jax
import jax.numpy as jnp
from jax import lax
from jax.experimental import pallas as pl
from jax.experimental.pallas import tpu as pltpu
from jax.sharding import PartitionSpec as P

MESH = pl.DeviceIdType.MESH
CHUNKS = 2
GROUP = 4


def gradient_kernel(
    rows, cols, count, back_hbm, weight_hbm, blocks_hbm, observed_hbm,
    out_ref, back_ref, weight_ref, states, blocks, misfit, block_sems, other_sems,
):
    block_total = rows.shape[1]
    row_size = blocks.shape[0] // block_total
    members = back_ref.shape[1]
    state_total, _, col_size = states.shape
    chunk = block_total // CHUNKS

    back_copy = pltpu.make_async_copy(back_hbm, back_ref, other_sems.at[0])
    observed_copy = pltpu.make_async_copy(observed_hbm, misfit, other_sems.at[1])
    weight_copy = pltpu.make_async_copy(weight_hbm, weight_ref, other_sems.at[2])
    back_copy.start()
    observed_copy.start()
    for part in range(CHUNKS):
        span = pl.ds(part * chunk * row_size, chunk * row_size)
        pltpu.make_async_copy(blocks_hbm.at[span], blocks.at[span], block_sems.at[part]).start()
    weight_copy.start()

    back_copy.wait()
    for k in range(state_total):
        states[k] = back_ref[0, :, k * col_size:(k + 1) * col_size]
    out_ref[...] = jnp.zeros_like(out_ref)
    lane_half = lax.broadcasted_iota(jnp.int32, (members, 2 * row_size), 1) // row_size
    in_use = count[0]
    observed_copy.wait()

    def place(row):
        return pl.ds(pl.multiple_of(lax.shift_right_logical(row, 1) * (2 * row_size), 2 * row_size), 2 * row_size)

    batch = chunk // GROUP

    def tile_of(group):
        span = GROUP * row_size
        return blocks[pl.ds(pl.multiple_of(group * span, span), span), :]

    def apply_batch(part, _):
        pltpu.make_async_copy(
            blocks_hbm.at[pl.ds(0, chunk * row_size)],
            blocks.at[pl.ds(0, chunk * row_size)],
            block_sems.at[part],
        ).wait()
        results = []
        for g in range(batch):
            first = part * chunk + g * GROUP
            picked = jnp.concatenate([states[cols[0, first + j]] for j in range(GROUP)], axis=0)
            results.append(lax.dot_general(
                picked, tile_of(part * batch + g), (((1,), (1,)), ((), ())),
                preferred_element_type=jnp.float32,
            ))
        for g in range(batch):
            first = part * chunk + g * GROUP
            for j in range(GROUP):
                row = rows[0, first + j]
                half = row & 1
                piece = results[g][
                    j * members:(j + 1) * members,
                    (j // 2) * 2 * row_size:(j // 2 + 1) * 2 * row_size,
                ]
                piece = pltpu.roll(piece, (half ^ (j % 2)) * row_size, 1)
                wanted = jnp.where(first + j < in_use, half, 2)
                at = place(row)
                misfit[:, at] = misfit[:, at] - jnp.where(lane_half == wanted, piece, 0.0)
        return 0

    lax.fori_loop(0, CHUNKS, apply_batch, 0)
    weight_copy.wait()

    def pull_batch(part, _):
        results = []
        for g in range(batch):
            first = part * chunk + g * GROUP
            pieces = []
            for j in range(GROUP):
                row = rows[0, first + j]
                at = place(row)
                value = misfit[:, at] * weight_ref[:, at]
                value = pltpu.roll(value, ((row & 1) ^ (j % 2)) * row_size, 1)
                wanted = jnp.where(first + j < in_use, j % 2, 2)
                value = jnp.where(lane_half == wanted, value, 0.0).astype(jnp.bfloat16)
                nothing = jnp.zeros_like(value)
                pieces.append(jnp.concatenate(
                    [value if s == j // 2 else nothing for s in range(GROUP // 2)], axis=1
                ))
            results.append(jnp.dot(
                jnp.concatenate(pieces, axis=0), tile_of(part * batch + g),
                preferred_element_type=jnp.float32,
            ))
        for g in range(batch):
            first = part * chunk + g * GROUP
            for j in range(GROUP):
                k = cols[0, first + j]
                out_ref[k] = out_ref[k] + results[g][j * members:(j + 1) * members]
        return 0

    lax.fori_loop(0, CHUNKS, pull_batch, 0)


def gradients(obs_blocks, block_rows, block_cols, block_count, background, observed, obs_weight):
    _, block_total, row_size, col_size = obs_blocks.shape
    members = background.shape[1]
    state_total = background.shape[2] // col_size
    smem = pl.BlockSpec(memory_space=pltpu.SMEM)
    vmem = pl.BlockSpec(memory_space=pltpu.VMEM)
    hbm = pl.BlockSpec(memory_space=pltpu.HBM)
    return pl.pallas_call(
        gradient_kernel,
        out_shape=jax.ShapeDtypeStruct((state_total, members, col_size), jnp.float32),
        in_specs=[smem, smem, smem, hbm, hbm, hbm, hbm],
        out_specs=vmem,
        scratch_shapes=[
            pltpu.VMEM(background.shape, jnp.bfloat16),
            pltpu.VMEM(obs_weight.shape, jnp.float32),
            pltpu.VMEM((state_total, members, col_size), jnp.bfloat16),
            pltpu.VMEM((block_total * row_size, col_size), jnp.bfloat16),
            pltpu.VMEM((members, observed.shape[2]), jnp.float32),
            pltpu.SemaphoreType.DMA((CHUNKS,)),
            pltpu.SemaphoreType.DMA((3,)),
        ],
        compiler_params=pltpu.CompilerParams(vmem_limit_bytes=62 * 2**20),
        name="local_gradient",
    )(
        block_rows, block_cols, block_count, background, obs_weight,
        obs_blocks.reshape(block_total * row_size, col_size),
        observed.reshape(members, observed.shape[2]),
    )


def smoother_kernel(
    n, grad_ref, info_ref, decay_ref, noise_ref, prior_ref, out,
    coef_send, coef_recv, grad_recv, mean_send, var_send,
    coef_ss, coef_rs, grad_ss, grad_rs, mean_ss, mean_rs, var_ss, var_rs, own_sems,
):
    me = lax.axis_index("tm")
    width = coef_send.shape[2]
    members = mean_send.shape[1]

    barrier = pltpu.get_barrier_semaphore()

    def greet(d, _):
        pl.semaphore_signal(
            barrier, inc=1, device_id={"tm": lax.rem(me + d, n)}, device_id_type=MESH
        )
        return 0

    lax.fori_loop(1, n, greet, 0)
    own_grad = pltpu.make_async_copy(grad_ref.at[me], grad_recv.at[me], own_sems.at[0])
    own_grad.start()
    for k in range(n):
        columns = slice(k * width, (k + 1) * width)
        coef_send[k] = jnp.concatenate(
            [info_ref[:, columns], decay_ref[:, columns], noise_ref[:, columns],
             jnp.zeros((1, width), jnp.float32)], axis=0
        )
    mine = pl.ds(pl.multiple_of(me * width, width), width)
    coef_recv[me] = coef_send[me]
    pl.semaphore_wait(barrier, n - 1)

    def start_all(src, dst, send_sem, recv_sem):
        def body(i, _):
            d = n // 2 + i
            to = lax.rem(me + jnp.where(d < n, d, d - n + 1), n)
            pltpu.make_async_remote_copy(
                src_ref=src.at[to], dst_ref=dst(me), send_sem=send_sem, recv_sem=recv_sem,
                device_id={"tm": to}, device_id_type=MESH,
            ).start()
            return 0
        lax.fori_loop(0, n - 1, body, 0)

    def everything(src, whole, send_sem, recv_sem):
        return pltpu.make_async_remote_copy(
            src_ref=src.at[pl.ds(0, n - 1)], dst_ref=whole, send_sem=send_sem, recv_sem=recv_sem,
            device_id={"tm": lax.rem(me + 1, n)}, device_id_type=MESH,
        )

    def columns_of(first, last):
        return lambda k: out.at[
            first:last, pl.ds(pl.multiple_of(k * width, width), width)
        ]

    start_all(coef_send, lambda k: coef_recv.at[k], coef_ss, coef_rs)
    start_all(grad_ref, lambda k: grad_recv.at[k], grad_ss, grad_rs)
    others = pl.ds(0, (n - 1) * width)
    coefs = everything(coef_send, coef_recv.at[pl.ds(0, n - 1)], coef_ss, coef_rs)
    grads = everything(grad_ref, grad_recv.at[pl.ds(0, n - 1)], grad_ss, grad_rs)
    means = everything(mean_send, out.at[0:members, others], mean_ss, mean_rs)
    varis = everything(var_send, out.at[members:members + 1, others], var_ss, var_rs)
    coefs.wait_recv()

    info = [coef_recv[t, 0:1, :] for t in range(n)]
    decay = [coef_recv[t, 1:2, :] for t in range(n)]
    noise = [coef_recv[t, 2:3, :] for t in range(n)]
    var, carry = [], []
    for t in range(n):
        if t == 0:
            pred = prior_ref[:, mine]
            carry.append(None)
        else:
            pred = decay[t] * decay[t] * var[t - 1] + noise[t]
        scale = 1.0 / (1.0 + info[t] * pred)
        var.append(pred * scale)
        if t > 0:
            carry.append(scale * decay[t])
    gain = []
    later = [None] * n
    later[n - 1] = var[n - 1]
    for t in range(n - 1):
        pred = decay[t + 1] * decay[t + 1] * var[t] + noise[t + 1]
        gain.append(var[t] * decay[t + 1] / pred)
    for t in range(n - 2, -1, -1):
        pred = decay[t + 1] * decay[t + 1] * var[t] + noise[t + 1]
        later[t] = var[t] + gain[t] * gain[t] * (later[t + 1] - pred)
    for t in range(n):
        var_send[t] = later[t]
    start_all(var_send, columns_of(members, members + 1), var_ss, var_rs)
    own_var = pltpu.make_async_copy(
        var_send.at[me], columns_of(members, members + 1)(me), own_sems.at[1]
    )
    own_var.start()

    own_grad.wait()
    grads.wait_recv()
    mean = []
    for t in range(n):
        now = var[t] * grad_recv[t]
        mean.append(now if t == 0 else carry[t] * mean[t - 1] + now)
    smooth = mean[n - 1]
    mean_send[n - 1] = smooth
    for t in range(n - 2, -1, -1):
        smooth = mean[t] + gain[t] * (smooth - decay[t + 1] * mean[t])
        mean_send[t] = smooth
    start_all(mean_send, columns_of(0, members), mean_ss, mean_rs)
    own_mean = pltpu.make_async_copy(mean_send.at[me], columns_of(0, members)(me), own_sems.at[2])
    own_mean.start()

    own_var.wait()
    own_mean.wait()
    varis.wait_recv()
    means.wait_recv()
    coefs.wait_send()
    grads.wait_send()
    varis.wait_send()
    means.wait_send()


def split_kernel(both, mean_out, var_out, sems):
    members = mean_out.shape[1]
    mean_copy = pltpu.make_async_copy(both.at[0:members], mean_out.at[0], sems.at[0])
    var_copy = pltpu.make_async_copy(both.at[members:members + 1], var_out, sems.at[1])
    mean_copy.start()
    var_copy.start()
    mean_copy.wait()
    var_copy.wait()


def exchange_and_smooth(n, gradient, info_diag, decay, noise_var, prior_var):
    state_total, members, width = gradient.shape
    total = state_total * width
    vmem = pl.BlockSpec(memory_space=pltpu.VMEM)
    hbm = pl.BlockSpec(memory_space=pltpu.HBM)
    out = pl.pallas_call(
        functools.partial(smoother_kernel, n),
        out_shape=jax.ShapeDtypeStruct((members + 1, total), jnp.float32),
        in_specs=[hbm] + [vmem] * 4,
        out_specs=pl.BlockSpec(memory_space=pl.ANY),
        scratch_shapes=[
            pltpu.VMEM((n, 4, width), jnp.float32),
            pltpu.VMEM((n, 4, width), jnp.float32),
            pltpu.VMEM((n, members, width), jnp.float32),
            pltpu.VMEM((n, members, width), jnp.float32),
            pltpu.VMEM((n, 1, width), jnp.float32),
        ] + [pltpu.SemaphoreType.DMA] * 8 + [pltpu.SemaphoreType.DMA((3,))],
        compiler_params=pltpu.CompilerParams(collective_id=0, has_side_effects=True, vmem_limit_bytes=8 * 2**20),
        name="exchange_smooth",
    )(gradient, info_diag, decay, noise_var, prior_var.reshape(1, total))
    return pl.pallas_call(
        split_kernel,
        out_shape=(
            jax.ShapeDtypeStruct((1, members, total), jnp.float32),
            jax.ShapeDtypeStruct((1, total), jnp.float32),
        ),
        in_specs=[pl.BlockSpec(memory_space=pl.ANY)],
        out_specs=(hbm, hbm),
        scratch_shapes=[pltpu.SemaphoreType.DMA((2,))],
        compiler_params=pltpu.CompilerParams(vmem_limit_bytes=8 * 2**20),
        name="split_outputs",
    )(out)


def sequential_smoother(series, prior_here, member_total):
    full_steps = series.shape[0]
    grad_all = series[:, :member_total, :]
    info_all = series[:, member_total, :]
    decay_all = series[:, member_total + 1, :]
    noise_all = series[:, member_total + 2, :]
    local_width = series.shape[2]
    step_ids = jnp.arange(full_steps)
    first_flags = step_ids == 0
    final_flags = step_ids == full_steps - 1

    def forward(carried, inputs):
        mean_prev, var_prev = carried
        grad_now, info_now, decay_now, noise_now, first_now = inputs
        pred_var = jnp.where(first_now, prior_here, decay_now * decay_now * var_prev + noise_now)
        pred_mean = jnp.where(first_now, 0.0, decay_now * mean_prev)
        var_now = pred_var / (1.0 + info_now * pred_var)
        mean_now = var_now * (pred_mean / pred_var + grad_now)
        return ((mean_now, var_now), (mean_now, var_now))

    initial = (
        jnp.zeros((member_total, local_width), jnp.float32),
        jnp.ones((local_width,), jnp.float32),
    )
    means, variances = lax.scan(
        forward, initial, (grad_all, info_all, decay_all, noise_all, first_flags)
    )[1]
    next_decay = jnp.concatenate([decay_all[1:], jnp.zeros((1, local_width), jnp.float32)], axis=0)
    next_noise = jnp.concatenate([noise_all[1:], jnp.ones((1, local_width), jnp.float32)], axis=0)

    def backward(carried, inputs):
        later_mean, later_var = carried
        mean_now, var_now, decay_next, noise_next, final_now = inputs
        pred_var = decay_next * decay_next * var_now + noise_next
        smoother_gain = jnp.where(final_now, 0.0, var_now * decay_next / pred_var)
        out_mean = mean_now + smoother_gain * (later_mean - decay_next * mean_now)
        out_var = var_now + smoother_gain * smoother_gain * (later_var - pred_var)
        return ((out_mean, out_var), (out_mean, out_var))

    closing = (
        jnp.zeros((member_total, local_width), jnp.float32),
        jnp.zeros((local_width,), jnp.float32),
    )
    return lax.scan(
        backward, closing, (means, variances, next_decay, next_noise, final_flags), reverse=True
    )[1]


def shards(
    obs_blocks,
    block_rows,
    block_cols,
    block_count,
    background,
    observed,
    obs_weight,
    info_diag,
    decay,
    noise_var,
    prior_var,
):
    member_total = background.shape[1]
    state_total = background.shape[2]
    n = lax.axis_size("tm")
    gradient = gradients(
        obs_blocks, block_rows, block_cols, block_count, background, observed, obs_weight
    )
    local_width = state_total // n
    if local_width == gradient.shape[2]:
        return exchange_and_smooth(n, gradient, info_diag, decay, noise_var, prior_var)
    gradient = jnp.transpose(gradient, (1, 0, 2)).reshape(1, member_total, state_total)
    packed = jnp.concatenate(
        [gradient, info_diag[:, None, :], decay[:, None, :], noise_var[:, None, :]], axis=1
    )
    series = lax.all_to_all(packed, "tm", split_axis=2, concat_axis=0, tiled=True)
    prior_here = lax.dynamic_slice_in_dim(
        prior_var, lax.axis_index("tm") * local_width, local_width, 0
    )
    mean_series, var_series = sequential_smoother(series, prior_here, member_total)
    outgoing = jnp.concatenate([mean_series, var_series[:, None, :]], axis=1)
    returned = lax.all_to_all(outgoing, "tm", split_axis=0, concat_axis=2, tiled=True)
    return (returned[:, :member_total, :], returned[:, member_total, :])


def solution(mesh):
    in_specs = (
        P(("group", "tm"), None, None, None),
        P(("group", "tm"), None),
        P(("group", "tm"), None),
        P(("group", "tm")),
        P(("group", "tm"), None, None),
        P(("group", "tm"), None, None),
        P(("group", "tm"), None),
        P(("group", "tm"), None),
        P(("group", "tm"), None),
        P(("group", "tm"), None),
        P("group"),
    )
    out_specs = (P(("group", "tm"), None, None), P(("group", "tm"), None))
    return jax.shard_map(shards, mesh=mesh, in_specs=in_specs, out_specs=out_specs, check_vma=False)
```

```python
import functools

import jax
import jax.numpy as jnp
from jax import lax
from jax.experimental import pallas as pl
from jax.experimental.pallas import tpu as pltpu
from jax.sharding import PartitionSpec as P

MESH = pl.DeviceIdType.MESH
CHUNKS = 2
GROUP = 4


def gradient_kernel(
    rows, cols, count, back_hbm, weight_hbm, blocks_hbm, observed_hbm,
    out_ref, back_ref, weight_ref, states, blocks, misfit, block_sems, other_sems,
):
    block_total = rows.shape[1]
    row_size = blocks.shape[0] // block_total
    members = back_ref.shape[1]
    state_total, _, col_size = states.shape
    chunk = block_total // CHUNKS

    back_copy = pltpu.make_async_copy(back_hbm, back_ref, other_sems.at[0])
    observed_copy = pltpu.make_async_copy(observed_hbm, misfit, other_sems.at[1])
    weight_copy = pltpu.make_async_copy(weight_hbm, weight_ref, other_sems.at[2])
    back_copy.start()
    observed_copy.start()
    for part in range(CHUNKS):
        span = pl.ds(part * chunk * row_size, chunk * row_size)
        pltpu.make_async_copy(blocks_hbm.at[span], blocks.at[span], block_sems.at[part]).start()
    weight_copy.start()

    back_copy.wait()
    for k in range(state_total):
        states[k] = back_ref[0, :, k * col_size:(k + 1) * col_size]
    out_ref[...] = jnp.zeros_like(out_ref)
    lane_half = lax.broadcasted_iota(jnp.int32, (members, 2 * row_size), 1) // row_size
    in_use = count[0]
    observed_copy.wait()

    def place(row):
        return pl.ds(pl.multiple_of(lax.shift_right_logical(row, 1) * (2 * row_size), 2 * row_size), 2 * row_size)

    batch = chunk // GROUP

    def tile_of(group):
        span = GROUP * row_size
        return blocks[pl.ds(pl.multiple_of(group * span, span), span), :]

    def apply_batch(part, _):
        pltpu.make_async_copy(
            blocks_hbm.at[pl.ds(0, chunk * row_size)],
            blocks.at[pl.ds(0, chunk * row_size)],
            block_sems.at[part],
        ).wait()
        results = []
        for g in range(batch):
            first = part * chunk + g * GROUP
            picked = jnp.concatenate([states[cols[0, first + j]] for j in range(GROUP)], axis=0)
            results.append(lax.dot_general(
                picked, tile_of(part * batch + g), (((1,), (1,)), ((), ())),
                preferred_element_type=jnp.float32,
            ))
        for g in range(batch):
            first = part * chunk + g * GROUP
            for j in range(GROUP):
                row = rows[0, first + j]
                half = row & 1
                piece = results[g][
                    j * members:(j + 1) * members,
                    (j // 2) * 2 * row_size:(j // 2 + 1) * 2 * row_size,
                ]
                piece = pltpu.roll(piece, (half ^ (j % 2)) * row_size, 1)
                wanted = jnp.where(first + j < in_use, half, 2)
                at = place(row)
                misfit[:, at] = misfit[:, at] - jnp.where(lane_half == wanted, piece, 0.0)
        return 0

    lax.fori_loop(0, CHUNKS, apply_batch, 0)
    weight_copy.wait()

    def pull_batch(part, _):
        results = []
        for g in range(batch):
            first = part * chunk + g * GROUP
            pieces = []
            for j in range(GROUP):
                row = rows[0, first + j]
                at = place(row)
                value = misfit[:, at] * weight_ref[:, at]
                value = pltpu.roll(value, ((row & 1) ^ (j % 2)) * row_size, 1)
                wanted = jnp.where(first + j < in_use, j % 2, 2)
                value = jnp.where(lane_half == wanted, value, 0.0).astype(jnp.bfloat16)
                nothing = jnp.zeros_like(value)
                pieces.append(jnp.concatenate(
                    [value if s == j // 2 else nothing for s in range(GROUP // 2)], axis=1
                ))
            results.append(jnp.dot(
                jnp.concatenate(pieces, axis=0), tile_of(part * batch + g),
                preferred_element_type=jnp.float32,
            ))
        for g in range(batch):
            first = part * chunk + g * GROUP
            for j in range(GROUP):
                k = cols[0, first + j]
                out_ref[k] = out_ref[k] + results[g][j * members:(j + 1) * members]
        return 0

    lax.fori_loop(0, CHUNKS, pull_batch, 0)


def gradients(obs_blocks, block_rows, block_cols, block_count, background, observed, obs_weight):
    _, block_total, row_size, col_size = obs_blocks.shape
    members = background.shape[1]
    state_total = background.shape[2] // col_size
    smem = pl.BlockSpec(memory_space=pltpu.SMEM)
    vmem = pl.BlockSpec(memory_space=pltpu.VMEM)
    hbm = pl.BlockSpec(memory_space=pltpu.HBM)
    return pl.pallas_call(
        gradient_kernel,
        out_shape=jax.ShapeDtypeStruct((state_total, members, col_size), jnp.float32),
        in_specs=[smem, smem, smem, hbm, hbm, hbm, hbm],
        out_specs=vmem,
        scratch_shapes=[
            pltpu.VMEM(background.shape, jnp.bfloat16),
            pltpu.VMEM(obs_weight.shape, jnp.float32),
            pltpu.VMEM((state_total, members, col_size), jnp.bfloat16),
            pltpu.VMEM((block_total * row_size, col_size), jnp.bfloat16),
            pltpu.VMEM((members, observed.shape[2]), jnp.float32),
            pltpu.SemaphoreType.DMA((CHUNKS,)),
            pltpu.SemaphoreType.DMA((3,)),
        ],
        compiler_params=pltpu.CompilerParams(vmem_limit_bytes=62 * 2**20),
        name="local_gradient",
    )(
        block_rows, block_cols, block_count, background, obs_weight,
        obs_blocks.reshape(block_total * row_size, col_size),
        observed.reshape(members, observed.shape[2]),
    )


def smoother_kernel(
    n, grad_ref, info_ref, decay_ref, noise_ref, prior_ref, out,
    coef_send, coef_recv, grad_recv, mean_send, var_send,
    coef_ss, coef_rs, grad_ss, grad_rs, mean_ss, mean_rs, var_ss, var_rs, own_sems,
):
    me = lax.axis_index("tm")
    width = coef_send.shape[2]
    members = mean_send.shape[1]

    barrier = pltpu.get_barrier_semaphore()

    def greet(d, _):
        pl.semaphore_signal(
            barrier, inc=1, device_id={"tm": lax.rem(me + d, n)}, device_id_type=MESH
        )
        return 0

    lax.fori_loop(1, n, greet, 0)
    own_grad = pltpu.make_async_copy(grad_ref.at[me], grad_recv.at[me], own_sems.at[0])
    own_grad.start()
    for k in range(n):
        columns = slice(k * width, (k + 1) * width)
        coef_send[k] = jnp.concatenate(
            [info_ref[:, columns], decay_ref[:, columns], noise_ref[:, columns],
             jnp.zeros((1, width), jnp.float32)], axis=0
        )
    mine = pl.ds(pl.multiple_of(me * width, width), width)
    coef_recv[me] = coef_send[me]
    pl.semaphore_wait(barrier, n - 1)

    def start_all(src, dst, send_sem, recv_sem):
        def body(i, _):
            d = n // 2 + i
            to = lax.rem(me + jnp.where(d < n, d, d - n + 1), n)
            pltpu.make_async_remote_copy(
                src_ref=src.at[to], dst_ref=dst(me), send_sem=send_sem, recv_sem=recv_sem,
                device_id={"tm": to}, device_id_type=MESH,
            ).start()
            return 0
        lax.fori_loop(0, n - 1, body, 0, unroll=5)

    def everything(src, whole, send_sem, recv_sem):
        return pltpu.make_async_remote_copy(
            src_ref=src.at[pl.ds(0, n - 1)], dst_ref=whole, send_sem=send_sem, recv_sem=recv_sem,
            device_id={"tm": lax.rem(me + 1, n)}, device_id_type=MESH,
        )

    def columns_of(first, last):
        return lambda k: out.at[
            first:last, pl.ds(pl.multiple_of(k * width, width), width)
        ]

    start_all(coef_send, lambda k: coef_recv.at[k], coef_ss, coef_rs)
    start_all(grad_ref, lambda k: grad_recv.at[k], grad_ss, grad_rs)
    others = pl.ds(0, (n - 1) * width)
    coefs = everything(coef_send, coef_recv.at[pl.ds(0, n - 1)], coef_ss, coef_rs)
    grads = everything(grad_ref, grad_recv.at[pl.ds(0, n - 1)], grad_ss, grad_rs)
    means = everything(mean_send, out.at[0:members, others], mean_ss, mean_rs)
    varis = everything(var_send, out.at[members:members + 1, others], var_ss, var_rs)
    coefs.wait_recv()

    info = [coef_recv[t, 0:1, :] for t in range(n)]
    decay = [coef_recv[t, 1:2, :] for t in range(n)]
    noise = [coef_recv[t, 2:3, :] for t in range(n)]
    var, carry = [], []
    for t in range(n):
        if t == 0:
            pred = prior_ref[:, mine]
            carry.append(None)
        else:
            pred = decay[t] * decay[t] * var[t - 1] + noise[t]
        scale = 1.0 / (1.0 + info[t] * pred)
        var.append(pred * scale)
        if t > 0:
            carry.append(scale * decay[t])
    gain = []
    later = [None] * n
    later[n - 1] = var[n - 1]
    for t in range(n - 1):
        pred = decay[t + 1] * decay[t + 1] * var[t] + noise[t + 1]
        gain.append(var[t] * decay[t + 1] / pred)
    for t in range(n - 2, -1, -1):
        pred = decay[t + 1] * decay[t + 1] * var[t] + noise[t + 1]
        later[t] = var[t] + gain[t] * gain[t] * (later[t + 1] - pred)
    for t in range(n):
        var_send[t] = later[t]
    start_all(var_send, columns_of(members, members + 1), var_ss, var_rs)
    own_var = pltpu.make_async_copy(
        var_send.at[me], columns_of(members, members + 1)(me), own_sems.at[1]
    )
    own_var.start()

    own_grad.wait()
    grads.wait_recv()
    mean = []
    for t in range(n):
        now = var[t] * grad_recv[t]
        mean.append(now if t == 0 else carry[t] * mean[t - 1] + now)
    smooth = mean[n - 1]
    mean_send[n - 1] = smooth
    for t in range(n - 2, -1, -1):
        smooth = mean[t] + gain[t] * (smooth - decay[t + 1] * mean[t])
        mean_send[t] = smooth
    start_all(mean_send, columns_of(0, members), mean_ss, mean_rs)
    own_mean = pltpu.make_async_copy(mean_send.at[me], columns_of(0, members)(me), own_sems.at[2])
    own_mean.start()

    own_var.wait()
    own_mean.wait()
    varis.wait_recv()
    means.wait_recv()
    coefs.wait_send()
    grads.wait_send()
    varis.wait_send()
    means.wait_send()


def split_kernel(both, mean_out, var_out, sems):
    members = mean_out.shape[1]
    mean_copy = pltpu.make_async_copy(both.at[0:members], mean_out.at[0], sems.at[0])
    var_copy = pltpu.make_async_copy(both.at[members:members + 1], var_out, sems.at[1])
    mean_copy.start()
    var_copy.start()
    mean_copy.wait()
    var_copy.wait()


def exchange_and_smooth(n, gradient, info_diag, decay, noise_var, prior_var):
    state_total, members, width = gradient.shape
    total = state_total * width
    vmem = pl.BlockSpec(memory_space=pltpu.VMEM)
    hbm = pl.BlockSpec(memory_space=pltpu.HBM)
    out = pl.pallas_call(
        functools.partial(smoother_kernel, n),
        out_shape=jax.ShapeDtypeStruct((members + 1, total), jnp.float32),
        in_specs=[hbm] + [vmem] * 4,
        out_specs=pl.BlockSpec(memory_space=pl.ANY),
        scratch_shapes=[
            pltpu.VMEM((n, 4, width), jnp.float32),
            pltpu.VMEM((n, 4, width), jnp.float32),
            pltpu.VMEM((n, members, width), jnp.float32),
            pltpu.VMEM((n, members, width), jnp.float32),
            pltpu.VMEM((n, 1, width), jnp.float32),
        ] + [pltpu.SemaphoreType.DMA] * 8 + [pltpu.SemaphoreType.DMA((3,))],
        compiler_params=pltpu.CompilerParams(collective_id=0, has_side_effects=True, vmem_limit_bytes=8 * 2**20),
        name="exchange_smooth",
    )(gradient, info_diag, decay, noise_var, prior_var.reshape(1, total))
    return pl.pallas_call(
        split_kernel,
        out_shape=(
            jax.ShapeDtypeStruct((1, members, total), jnp.float32),
            jax.ShapeDtypeStruct((1, total), jnp.float32),
        ),
        in_specs=[pl.BlockSpec(memory_space=pl.ANY)],
        out_specs=(hbm, hbm),
        scratch_shapes=[pltpu.SemaphoreType.DMA((2,))],
        compiler_params=pltpu.CompilerParams(vmem_limit_bytes=8 * 2**20),
        name="split_outputs",
    )(out)


def sequential_smoother(series, prior_here, member_total):
    full_steps = series.shape[0]
    grad_all = series[:, :member_total, :]
    info_all = series[:, member_total, :]
    decay_all = series[:, member_total + 1, :]
    noise_all = series[:, member_total + 2, :]
    local_width = series.shape[2]
    step_ids = jnp.arange(full_steps)
    first_flags = step_ids == 0
    final_flags = step_ids == full_steps - 1

    def forward(carried, inputs):
        mean_prev, var_prev = carried
        grad_now, info_now, decay_now, noise_now, first_now = inputs
        pred_var = jnp.where(first_now, prior_here, decay_now * decay_now * var_prev + noise_now)
        pred_mean = jnp.where(first_now, 0.0, decay_now * mean_prev)
        var_now = pred_var / (1.0 + info_now * pred_var)
        mean_now = var_now * (pred_mean / pred_var + grad_now)
        return ((mean_now, var_now), (mean_now, var_now))

    initial = (
        jnp.zeros((member_total, local_width), jnp.float32),
        jnp.ones((local_width,), jnp.float32),
    )
    means, variances = lax.scan(
        forward, initial, (grad_all, info_all, decay_all, noise_all, first_flags)
    )[1]
    next_decay = jnp.concatenate([decay_all[1:], jnp.zeros((1, local_width), jnp.float32)], axis=0)
    next_noise = jnp.concatenate([noise_all[1:], jnp.ones((1, local_width), jnp.float32)], axis=0)

    def backward(carried, inputs):
        later_mean, later_var = carried
        mean_now, var_now, decay_next, noise_next, final_now = inputs
        pred_var = decay_next * decay_next * var_now + noise_next
        smoother_gain = jnp.where(final_now, 0.0, var_now * decay_next / pred_var)
        out_mean = mean_now + smoother_gain * (later_mean - decay_next * mean_now)
        out_var = var_now + smoother_gain * smoother_gain * (later_var - pred_var)
        return ((out_mean, out_var), (out_mean, out_var))

    closing = (
        jnp.zeros((member_total, local_width), jnp.float32),
        jnp.zeros((local_width,), jnp.float32),
    )
    return lax.scan(
        backward, closing, (means, variances, next_decay, next_noise, final_flags), reverse=True
    )[1]


def shards(
    obs_blocks,
    block_rows,
    block_cols,
    block_count,
    background,
    observed,
    obs_weight,
    info_diag,
    decay,
    noise_var,
    prior_var,
):
    member_total = background.shape[1]
    state_total = background.shape[2]
    n = lax.axis_size("tm")
    gradient = gradients(
        obs_blocks, block_rows, block_cols, block_count, background, observed, obs_weight
    )
    local_width = state_total // n
    if local_width == gradient.shape[2]:
        return exchange_and_smooth(n, gradient, info_diag, decay, noise_var, prior_var)
    gradient = jnp.transpose(gradient, (1, 0, 2)).reshape(1, member_total, state_total)
    packed = jnp.concatenate(
        [gradient, info_diag[:, None, :], decay[:, None, :], noise_var[:, None, :]], axis=1
    )
    series = lax.all_to_all(packed, "tm", split_axis=2, concat_axis=0, tiled=True)
    prior_here = lax.dynamic_slice_in_dim(
        prior_var, lax.axis_index("tm") * local_width, local_width, 0
    )
    mean_series, var_series = sequential_smoother(series, prior_here, member_total)
    outgoing = jnp.concatenate([mean_series, var_series[:, None, :]], axis=1)
    returned = lax.all_to_all(outgoing, "tm", split_axis=0, concat_axis=2, tiled=True)
    return (returned[:, :member_total, :], returned[:, member_total, :])


def solution(mesh):
    in_specs = (
        P(("group", "tm"), None, None, None),
        P(("group", "tm"), None),
        P(("group", "tm"), None),
        P(("group", "tm")),
        P(("group", "tm"), None, None),
        P(("group", "tm"), None, None),
        P(("group", "tm"), None),
        P(("group", "tm"), None),
        P(("group", "tm"), None),
        P(("group", "tm"), None),
        P("group"),
    )
    out_specs = (P(("group", "tm"), None, None), P(("group", "tm"), None))
    return jax.shard_map(shards, mesh=mesh, in_specs=in_specs, out_specs=out_specs, check_vma=False)
```
